32 devices in a mesh: dp: 8 (over z, x), seq: 4 (over y, core).
Axes of the slice: x: 2, y: 2, z: 4, core: 2. Of those that a mesh axis runs over, the one named last changes fastest.
Arguments:
- hidden_states: bfloat16 [8, 512, 4096], P('dp', 'seq'), may hold values from -6 to 6
- queries: bfloat16 [8, 512, 4096], P('dp', 'seq'), may hold values from -20 to 20
- key_states: bfloat16 [8, 512, 512], P('dp', 'seq'), may hold values from -6 to 6
- context_grad: bfloat16 [8, 512, 4096], P('dp', 'seq'), may hold values from -6 to 6
- doc_lengths: int32 [8, 16], P('dp'), may hold values from 1 to 64, 512 in all within a row
- value_weight: bfloat16 [4096, 512], P('dp'), may hold values from -0.09375 to 0.09375
Outputs:
- hidden_grad: bfloat16 [8, 512, 4096], P('dp', 'seq')
- query_grad: bfloat16 [8, 512, 4096], P('dp', 'seq')
- key_grad: bfloat16 [8, 512, 512], P('dp', 'seq')
- value_weight_grad: float32 [4096, 512], P(('dp', 'seq'))
The draws below stay inside these ranges and needn't reach their ends.
Inputs may be any that keep to these rules, and one draw needn't show every extreme that they name: `doc_lengths`: row s holds the lengths of the 16 documents of sequence s in order; they sum to 512.
All inputs are finite; a program needn't handle non-finite values.
Results may differ from the reference program's by a relative error of at most 0.011.
Values may be sent and summed in bfloat16 or wider, within the bound.
A program may use at most 128 MiB of HBM per device.

```python
import math
import jax
import jax.numpy as jnp
import numpy as np
from jax import lax

D = 4096
H = 32
KV = 4
HD = 128
DOCS = 16
LEN = 512
SEQS = 8
DOC_MOST = 64


def draw_pair(key):
    shape_keys = (SEQS, LEN, KV * HD)
    shape_queries = (SEQS, LEN, H * HD)
    key_out = jnp.clip(jax.random.normal(jax.random.fold_in(key, 11), shape_keys, jnp.float32), -6.0, 6.0)
    query_out = jnp.clip(jax.random.normal(jax.random.fold_in(key, 12), shape_queries, jnp.float32), -6.0, 6.0)
    return (query_out, key_out)


def draw_queries(key, part):
    return draw_pair(key)[0].astype(jnp.bfloat16)


def draw_key_states(key, part):
    return draw_pair(key)[1].astype(jnp.bfloat16)


def with_spikes(result, key, source, target, blocks, factor):
    owner, partner = [(jnp.arange(result.shape[axis_at]) // (result.shape[axis_at] // blocks)).reshape([-1 if axis == axis_at else 1 for axis in range(result.ndim)]) for axis_at in (source, target)]
    chosen = jax.random.permutation(key, blocks)[partner]
    strong = (owner == chosen) | (owner == (partner + blocks // 2) % blocks)
    return jnp.where(strong, factor * result, result)


def block_levels(rng, extent, pieces, low, high):
    factor_of = 1.0
    for axis_at, parts in pieces:
        draws = jax.random.uniform(jax.random.fold_in(jax.random.fold_in(rng, 6), axis_at), (parts,), jnp.float32, low / len(pieces), high / len(pieces))
        factor_of = factor_of * jnp.repeat(jnp.exp(draws), extent[axis_at] // parts).reshape((-1,) + (1,) * (len(extent) - 1 - axis_at))
    return factor_of


def profile(number_of, total, limit, skew):
    loads = [(1 << 20) // math.isqrt(rank ** skew) + 1 for rank in range(2, number_of + 1)]
    rest, holding = total - limit - (number_of - 1), [1] * (number_of - 1)
    while rest > 0:
        candidates = [i for i in range(number_of - 1) if holding[i] < limit]
        whole, budget = sum([loads[i] for i in candidates]), rest
        for i in candidates:
            extra = min(limit - holding[i], max(1, budget * loads[i] // whole), rest)
            holding[i] = holding[i] + extra
            rest = rest - extra
    return np.array([limit] + holding)


def uneven(rng, amount, total, reach, skew):
    if amount == 2:
        one = jax.random.randint(rng, (), max(1, total - reach), min(reach, total - 1) + 1)
        return jnp.stack([one, total - one])
    tallies = jnp.asarray(profile(amount, total, reach, skew), jnp.int32)
    twos = (amount - 1) // 2
    donor, sink = tallies[1:1 + 2 * twos:2], tallies[2:2 + 2 * twos:2]
    room = jnp.minimum(donor - 1, reach - sink)
    shifted = jax.random.randint(jax.random.fold_in(rng, 1), (twos,), 0, 1 << 20) % (room + 1)
    tallies = tallies.at[1:1 + 2 * twos:2].set(donor - shifted).at[2:2 + 2 * twos:2].set(sink + shifted)
    return tallies[jax.random.permutation(jax.random.fold_in(rng, 2), amount)]


def gaussian(stream_key, dims, deviation, bound, pieces=(), kind=jnp.bfloat16):
    loudness = block_levels(stream_key, dims, pieces, -0.22, 0.18) if pieces else 1.0
    values = jax.random.normal(stream_key, dims, jnp.float32) * deviation * loudness
    return jnp.minimum(jnp.maximum(values, -bound), bound).astype(kind)


def gaussian_with(key, shape, scale, limit, split, heavy, kind=jnp.bfloat16):
    entries = scale * jax.random.normal(key, shape, jnp.float32)
    if split:
        entries = entries * block_levels(key, shape, split, -0.22, 0.18)
    return jnp.clip(with_spikes(entries, jax.random.fold_in(key, 3), *heavy), -limit, limit).astype(kind)


def setup_inputs(seed: int = 0) -> dict:
    key_list = jax.random.split(jax.random.key(seed), 7)
    return {
        "hidden_states": gaussian_with(key_list[0], (SEQS, LEN, D), 1.0, 6.0, ((0, 8), (1, 4)), (1, 2, 4, 2.0)),
        "queries": draw_queries(jax.random.fold_in(key_list[6], 71), 0),
        "key_states": draw_key_states(jax.random.fold_in(key_list[6], 71), 0),
        "context_grad": gaussian(key_list[3], (SEQS, LEN, H * HD), 1.0, 6.0, ((0, 8), (1, 4))),
        "doc_lengths": jax.vmap(lambda own: uneven(own, DOCS, LEN, DOC_MOST, 2))(jax.random.split(key_list[4], SEQS)).reshape((SEQS, DOCS)).astype(jnp.int32),
        "value_weight": gaussian(key_list[5], (D, KV * HD), D ** -0.5, 0.09375, ((0, 8),)),
    }


far_negative = -1.0e30


def segment_ids(lengths_row, length):
    doc_ends = jnp.cumsum(lengths_row).astype(jnp.int32)
    positions = jnp.arange(length, dtype=jnp.int32)
    return jnp.sum((positions[:, None] >= doc_ends[None, :]).astype(jnp.int32), axis=1).astype(jnp.int32)


def reference(hidden_states, queries, key_states, context_grad, doc_lengths, value_weight):
    group_size = H // KV
    score_scale = HD ** -0.5
    flat_hidden = hidden_states.reshape(SEQS * LEN, D)
    values = jnp.dot(flat_hidden, value_weight, preferred_element_type=jnp.float32).astype(jnp.bfloat16)
    values = values.reshape(SEQS, LEN, KV, HD)

    def one_sequence(packed):
        query_seq, key_seq, value_seq, grad_seq, lengths_row = packed
        segment = segment_ids(lengths_row, LEN)
        positions = jnp.arange(LEN, dtype=jnp.int32)
        allowed = (positions[None, :] <= positions[:, None]) & (segment[None, :] == segment[:, None])

        def one_group(grouped):
            query_grp, key_grp, value_grp, grad_grp = grouped
            query_f = query_grp.astype(jnp.float32)
            key_f = key_grp.astype(jnp.float32)
            value_f = value_grp.astype(jnp.float32)
            grad_f = grad_grp.astype(jnp.float32)
            scores = jnp.einsum('igd,jd->gij', query_f, key_f) * score_scale
            scores = jnp.where(allowed[None], scores, far_negative)
            row_peak = jnp.max(scores, axis=-1, keepdims=True)
            exponent = jnp.exp(scores - row_peak)
            softmax_weights = exponent / jnp.sum(exponent, axis=-1, keepdims=True)
            weights_low = softmax_weights.astype(jnp.bfloat16).astype(jnp.float32)
            attended = jnp.einsum('gij,jd->igd', weights_low, value_f)
            row_delta = jnp.sum(grad_f * attended, axis=-1)
            softmax_grad = jnp.einsum('igd,jd->gij', grad_f, value_f)
            score_grad = softmax_weights * (softmax_grad - jnp.transpose(row_delta)[:, :, None])
            score_low = score_grad.astype(jnp.bfloat16).astype(jnp.float32)
            query_out = (jnp.einsum('gij,jd->igd', score_low, key_f) * score_scale).astype(jnp.bfloat16)
            key_out = jnp.einsum('gij,igd->jd', score_low, query_f) * score_scale
            value_out = jnp.einsum('gij,igd->jd', weights_low, grad_f)
            return query_out, key_out, value_out

        query_groups = jnp.transpose(query_seq.reshape(LEN, KV, group_size, HD), (1, 0, 2, 3))
        grad_groups = jnp.transpose(grad_seq.reshape(LEN, KV, group_size, HD), (1, 0, 2, 3))
        key_groups = jnp.transpose(key_seq.reshape(LEN, KV, HD), (1, 0, 2))
        value_groups = jnp.transpose(value_seq, (1, 0, 2))
        query_out, key_out, value_out = lax.map(one_group, (query_groups, key_groups, value_groups, grad_groups))
        query_out = jnp.transpose(query_out, (1, 0, 2, 3)).reshape(LEN, H * HD)
        key_out = jnp.transpose(key_out, (1, 0, 2)).reshape(LEN, KV * HD)
        value_out = jnp.transpose(value_out, (1, 0, 2)).reshape(LEN, KV * HD)
        return query_out, key_out, value_out

    query_grad, key_sum, value_sum = lax.map(one_sequence, (queries, key_states, values, context_grad, doc_lengths))
    value_low = value_sum.astype(jnp.bfloat16).reshape(SEQS * LEN, KV * HD)
    hidden_grad = jnp.dot(value_low, value_weight.T, preferred_element_type=jnp.float32).astype(jnp.bfloat16)
    hidden_grad = hidden_grad.reshape(SEQS, LEN, D)
    value_weight_grad = jnp.dot(flat_hidden.T, value_low, preferred_element_type=jnp.float32)
    return hidden_grad, query_grad, key_sum.astype(jnp.bfloat16), value_weight_grad
```

```python
import functools

import jax
import jax.numpy as jnp
from jax import lax
from jax.experimental import pallas as pl
from jax.experimental.pallas import tpu as pltpu
from jax.sharding import PartitionSpec as P

HD = 128
FAR_NEGATIVE = -1e30
MESH = pl.DeviceIdType.MESH
BF16 = jnp.bfloat16
F32 = jnp.float32


def dot(a, b, ca, cb):
    return lax.dot_general(a, b, (((ca,), (cb,)), ((), ())), preferred_element_type=F32)


def kernel(
    sizes,
    hidden_ref,
    query_ref,
    key_ref,
    grad_ref,
    lengths_ref,
    weight_ref,
    hidden_grad_ref,
    query_grad_ref,
    key_grad_ref,
    weight_grad_ref,
    hs,
    hq,
    wq,
    kf,
    pv,
    pr,
    vf,
    ws,
    ka,
    kh,
    kr,
    vc,
    va,
    vl,
    gp,
    gs,
    xr,
    zs,
    zr,
    hg,
    hr,
    s_hid, r_hid, s_wz, s_wx, r_w, s_k, r_k, s_pv, r_pv, s_kg, r_kg,
    s_vc, r_vc, s_gx, r_gx, s_gz, r_gz, s_hg, r_hg,
):
    T, n_seq, n_dp, na, nb, halo, R, kv, group = sizes
    C = kv * HD
    Kw = halo + T
    L = n_seq * T
    scale = HD ** -0.5
    W = n_dp * R
    s = lax.axis_index("seq")
    d = lax.axis_index("dp")
    a, b = lax.div(d, nb), lax.rem(d, nb)
    seq_peers = [lax.rem(s + o, n_seq) for o in range(1, n_seq)]
    seq_from = [lax.rem(s + n_seq - o, n_seq) for o in range(1, n_seq)]
    a_peers = [lax.rem(a + o, na) for o in range(1, na)]
    a_from = [lax.rem(a + na - o, na) for o in range(1, na)]
    b_peers = [lax.rem(b + o, nb) for o in range(1, nb)]
    b_from = [lax.rem(b + nb - o, nb) for o in range(1, nb)]

    sends = []

    def rows(i, n):
        return pl.ds(pl.multiple_of(i * n, n), n)

    def copy(src, dst, ss, rs, where):
        return pltpu.make_async_remote_copy(
            src_ref=src, dst_ref=dst, send_sem=ss, recv_sem=rs, device_id=where, device_id_type=MESH
        )

    def start(*args):
        c = copy(*args)
        c.start()
        sends.append(c)

    barrier = pltpu.get_barrier_semaphore()
    for p in seq_peers:
        pl.semaphore_signal(barrier, inc=1, device_id={"seq": p}, device_id_type=MESH)
    for p in a_peers:
        pl.semaphore_signal(barrier, inc=1, device_id={"dp": p * nb + b}, device_id_type=MESH)
    for p in b_peers:
        pl.semaphore_signal(barrier, inc=1, device_id={"dp": a * nb + p}, device_id_type=MESH)

    kf[halo:, :] = key_ref[...]
    wq[rows(d, R), :] = weight_ref[rows(s, R), :]
    for t in range(n_seq):
        if R % 128 == 0:
            for e in range(n_dp):
                at = (e * n_seq + t) * R
                hs[t, :, e * R : (e + 1) * R] = hidden_ref[:, at : at + R]
        else:
            hs[t] = hidden_ref[t]

    pl.semaphore_wait(barrier, n_seq - 1 + na - 1 + nb - 1)

    def w_slot(i):
        return wq.at[rows(i, R), :]

    for o, p in enumerate(a_peers):
        start(w_slot(d), w_slot(d), s_wz.at[o], r_w.at[d], {"dp": p * nb + b})

    def pass_on(i, k):
        for o, p in enumerate(b_peers):
            start(w_slot(i), w_slot(i), s_wx.at[k, o], r_w.at[i], {"dp": a * nb + p})

    pass_on(d, 0)

    blocks = []
    left = halo
    while left > 0:
        m = min(T, left)
        blocks.append((left - m, m))
        left -= m
    for o, (at, m) in enumerate(blocks):
        start(
            key_ref.at[T - m :, :], kf.at[at : at + m, :], s_k.at[o], r_k.at[o],
            {"seq": lax.rem(s + o + 1, n_seq)},
        )
    for o, p in enumerate(seq_peers):
        start(hs.at[p], hq.at[rows(s, T), :], s_hid.at[o], r_hid.at[s], {"seq": p})
    hq[rows(s, T), :] = hs[s]

    query_at = s * T + lax.broadcasted_iota(jnp.int32, (Kw, T), 1)
    key_at = s * T - halo + lax.broadcasted_iota(jnp.int32, (Kw, T), 0)
    begin = jnp.zeros((Kw, T), jnp.int32)
    end = jnp.int32(0)
    for i in range(lengths_ref.shape[1]):
        end = end + lengths_ref[0, i]
        begin = jnp.where(query_at >= end, end, begin)
    seen = (key_at >= begin) & (key_at <= query_at)
    bias = jnp.where(seen, 0.0, FAR_NEGATIVE).astype(F32)

    for o, (at, m) in enumerate(blocks):
        copy(
            key_ref.at[T - m :, :], kf.at[at : at + m, :], s_k.at[o], r_k.at[o],
            {"seq": lax.rem(s + o + 1, n_seq)},
        ).wait_recv()

    def stack(ref, g):
        return jnp.concatenate(
            [ref[:, pl.ds(pl.multiple_of((g * group + h) * HD, HD), HD)] for h in range(group)], axis=0
        )

    def head(g):
        return pl.ds(pl.multiple_of(g * HD, HD), HD)

    def scores(g, _):
        qs = stack(query_ref, g)
        sc = dot(kf[:, head(g)], qs, 1, 1) * scale + jnp.concatenate([bias] * group, axis=1)
        e = jnp.exp(sc - jnp.max(sc, axis=0, keepdims=True))
        ws[g] = e / jnp.sum(e, axis=0, keepdims=True)
        return 0

    lax.fori_loop(0, kv, scores, 0)

    for k, p in enumerate(a_from):
        i = p * nb + b
        copy(w_slot(i), w_slot(i), s_wz.at[k], r_w.at[i], {"dp": d}).wait_recv()
        pass_on(i, k + 1)
    for o, p in enumerate(seq_from):
        copy(hs.at[p], hq.at[rows(p, T), :], s_hid.at[o], r_hid.at[p], {"seq": s}).wait_recv()
    for p in b_from:
        for z in range(na):
            i = z * nb + p
            copy(w_slot(i), w_slot(i), s_wz.at[0], r_w.at[i], {"dp": d}).wait_recv()

    pv[:halo, :] = jnp.zeros((halo, C), BF16)

    def project(t, _):
        pv[pl.ds(pl.multiple_of(halo + t * T, 16), T), :] = dot(hq[rows(t, T), :], wq[...], 1, 0).astype(BF16)
        return 0

    lax.fori_loop(0, n_seq, project, 0)

    def pv_rows(t):
        return pv.at[pl.ds(pl.multiple_of(t * T, T), Kw), :]

    for o, p in enumerate(seq_peers):
        start(pv_rows(p), pr.at[s], s_pv.at[o], r_pv.at[s], {"seq": p})
    pr[s] = pv[pl.ds(pl.multiple_of(s * T, T), Kw), :]
    for o, p in enumerate(seq_from):
        copy(pv_rows(p), pr.at[p], s_pv.at[o], r_pv.at[p], {"seq": s}).wait_recv()
    total = pr[0].astype(F32)
    for t in range(1, n_seq):
        total = total + pr[t].astype(F32)
    vf[...] = total.astype(BF16)

    def grads(g, _):
        qs = stack(query_ref, g)
        cs = stack(grad_ref, g)
        kg = kf[:, head(g)]
        w = ws[g]
        wl = w.astype(BF16)
        sg = dot(vf[:, head(g)], cs, 1, 1)
        delta = jnp.sum(wl.astype(F32) * sg, axis=0, keepdims=True)
        ds = (w * (sg - delta)).astype(BF16)
        vc[s, :, head(g)] = dot(wl, cs, 1, 0).astype(BF16)
        ka[:, head(g)] = dot(ds, qs, 1, 0) * scale
        qg = (dot(ds, kg, 0, 0) * scale).astype(BF16)
        for h in range(group):
            query_grad_ref[:, pl.ds(pl.multiple_of((g * group + h) * HD, HD), HD)] = qg[h * T : (h + 1) * T]
        return 0

    lax.fori_loop(0, kv, grads, 0)

    for o, p in enumerate(seq_peers):
        start(vc.at[s], vc.at[s], s_vc.at[o], r_vc.at[s], {"seq": p})
    kh[...] = ka[:halo, :].astype(BF16)
    for o, (at, m) in enumerate(blocks):
        start(
            kh.at[at : at + m, :], kr.at[at : at + m, :], s_kg.at[o], r_kg.at[o],
            {"seq": lax.rem(s + 2 * n_seq - o - 1, n_seq)},
        )
    va[...] = jnp.zeros((halo + L, C), F32)
    for o, p in enumerate(seq_from):
        copy(vc.at[p], vc.at[p], s_vc.at[o], r_vc.at[p], {"seq": s}).wait_recv()
    for t in range(n_seq):
        va[t * T : t * T + Kw, :] += vc[t].astype(F32)
    vl[...] = va[halo:, :].astype(BF16)

    part = min(W, 256)
    for c in range(0, W, part):
        x = dot(hq[:, c : c + part], vl[...], 0, 0)
        gp[c : c + part, :] = x
        gs[c : c + part, :] = x.astype(BF16)
    for k, z in enumerate(a_peers + [a]):
        for o, p in enumerate(b_peers):
            start(
                gs.at[rows(z * nb + p, R), :], xr.at[b, rows(z, R), :], s_gx.at[k, o], r_gx.at[b, z],
                {"dp": a * nb + p},
            )

    for o, p in enumerate(seq_peers + [s]):
        x = dot(vl[rows(p, T), :], wq[...], 1, 1).astype(BF16)
        if o < n_seq - 1:
            hg[p] = x
            start(hg.at[p], hr.at[s], s_hg.at[o], r_hg.at[s], {"seq": p})
        else:
            hr[s] = x

    def reduced(z):
        x = gp[rows(z * nb + b, R), :]
        for p in b_from:
            copy(
                gs.at[rows(z * nb + p, R), :], xr.at[p, rows(z, R), :], s_gx.at[0, 0], r_gx.at[p, z],
                {"dp": d},
            ).wait_recv()
            x = x + xr[p, rows(z, R), :].astype(F32)
        return x

    for o, z in enumerate(a_peers):
        zs[z] = reduced(z).astype(BF16)
        start(zs.at[z], zr.at[a], s_gz.at[o], r_gz.at[a], {"dp": z * nb + b})
    mine = reduced(a)

    for o, (at, m) in enumerate(blocks):
        copy(
            kh.at[at : at + m, :], kr.at[at : at + m, :], s_kg.at[o], r_kg.at[o], {"seq": s}
        ).wait_recv()
        ka[Kw - m :, :] += kr[at : at + m, :].astype(F32)
    key_grad_ref[...] = ka[halo:, :].astype(BF16)

    for o, p in enumerate(a_from):
        copy(zs.at[p], zr.at[p], s_gz.at[o], r_gz.at[p], {"dp": d}).wait_recv()
        mine = mine + zr[p].astype(F32)
    weight_grad_ref[...] = mine

    for o, p in enumerate(seq_from):
        copy(hg.at[p], hr.at[p], s_hg.at[o], r_hg.at[p], {"seq": s}).wait_recv()
    for t in range(n_seq):
        if R % 128 == 0:
            for e in range(n_dp):
                at = (e * n_seq + t) * R
                hidden_grad_ref[:, at : at + R] = hr[t, :, e * R : (e + 1) * R]
        else:
            hidden_grad_ref[t] = hr[t]
    for c in sends:
        c.wait_send()


def body(n_dp, n_seq, hidden_states, queries, key_states, context_grad, doc_lengths, value_weight):
    _, T, D = hidden_states.shape
    C = key_states.shape[2]
    kv = C // HD
    group = queries.shape[2] // C
    L = T * n_seq
    halo = min(L, L // 8)
    R = value_weight.shape[0] // n_seq
    na = 4 if n_dp % 4 == 0 else n_dp
    nb = n_dp // na
    W = n_dp * R
    Kw = halo + T
    n_halo = -(-halo // T)
    sizes = (T, n_seq, n_dp, na, nb, halo, R, kv, group)
    hidden = hidden_states[0]
    wide = R % 128 == 0
    if not wide:
        hidden = hidden.reshape(T, n_dp, n_seq, R).transpose(2, 0, 1, 3).reshape(n_seq, T, W)
    vmem = pl.BlockSpec(memory_space=pltpu.VMEM)
    sem = lambda *shape: pltpu.SemaphoreType.DMA(shape)
    out = pl.pallas_call(
        functools.partial(kernel, sizes),
        out_shape=(
            jax.ShapeDtypeStruct(hidden.shape, BF16),
            jax.ShapeDtypeStruct((T, queries.shape[2]), BF16),
            jax.ShapeDtypeStruct((T, C), BF16),
            jax.ShapeDtypeStruct((R, C), F32),
        ),
        in_specs=[vmem, vmem, vmem, vmem, pl.BlockSpec(memory_space=pltpu.SMEM), vmem],
        out_specs=(vmem,) * 4,
        scratch_shapes=[
            pltpu.VMEM((n_seq, T, W), BF16),
            pltpu.VMEM((L, W), BF16),
            pltpu.VMEM((W, C), BF16),
            pltpu.VMEM((Kw, C), BF16),
            pltpu.VMEM((halo + L, C), BF16),
            pltpu.VMEM((n_seq, Kw, C), BF16),
            pltpu.VMEM((Kw, C), BF16),
            pltpu.VMEM((kv, Kw, group * T), F32),
            pltpu.VMEM((Kw, C), F32),
            pltpu.VMEM((halo, C), BF16),
            pltpu.VMEM((halo, C), BF16),
            pltpu.VMEM((n_seq, Kw, C), BF16),
            pltpu.VMEM((halo + L, C), F32),
            pltpu.VMEM((L, C), BF16),
            pltpu.VMEM((W, C), F32),
            pltpu.VMEM((W, C), BF16),
            pltpu.VMEM((nb, na * R, C), BF16),
            pltpu.VMEM((na, R, C), BF16),
            pltpu.VMEM((na, R, C), BF16),
            pltpu.VMEM((n_seq, T, W), BF16),
            pltpu.VMEM((n_seq, T, W), BF16),
            sem(n_seq), sem(n_seq),
            sem(na), sem(na, nb), sem(n_dp),
            sem(n_halo), sem(n_halo),
            sem(n_seq), sem(n_seq),
            sem(n_halo), sem(n_halo),
            sem(n_seq), sem(n_seq),
            sem(na, nb), sem(nb, na),
            sem(na), sem(na),
            sem(n_seq), sem(n_seq),
        ],
        compiler_params=pltpu.CompilerParams(
            collective_id=0, has_side_effects=True, vmem_limit_bytes=56 * 1024 * 1024
        ),
        name="attention_backward",
    )(hidden, queries[0], key_states[0], context_grad[0], doc_lengths, value_weight)
    hidden_grad = out[0]
    if not wide:
        hidden_grad = hidden_grad.reshape(n_seq, T, n_dp, R).transpose(1, 2, 0, 3).reshape(T, D)
    return hidden_grad[None], out[1][None], out[2][None], out[3]


def solution(mesh):
    return jax.shard_map(
        functools.partial(body, mesh.shape["dp"], mesh.shape["seq"]),
        mesh=mesh,
        in_specs=(
            P("dp", "seq", None),
            P("dp", "seq", None),
            P("dp", "seq", None),
            P("dp", "seq", None),
            P("dp", None),
            P("dp", None),
        ),
        out_specs=(
            P("dp", "seq", None),
            P("dp", "seq", None),
            P("dp", "seq", None),
            P(("dp", "seq"), None),
        ),
        check_vma=False,
    )
```

```python
import functools

import jax
import jax.numpy as jnp
from jax import lax
from jax.experimental import pallas as pl
from jax.experimental.pallas import tpu as pltpu
from jax.sharding import PartitionSpec as P

HD = 128
FAR_NEGATIVE = -1e30
MESH = pl.DeviceIdType.MESH
BF16 = jnp.bfloat16
F32 = jnp.float32


def dot(a, b, ca, cb):
    return lax.dot_general(a, b, (((ca,), (cb,)), ((), ())), preferred_element_type=F32)


def kernel(
    sizes,
    hidden_any,
    query_any,
    key_ref,
    grad_any,
    lengths_ref,
    weight_ref,
    hidden_grad_ref,
    query_grad_any,
    key_grad_ref,
    weight_grad_ref,
    hid,
    query_ref,
    grad_ref,
    query_grad_ref,
    hs,
    hq,
    wq,
    kf,
    pv,
    pc,
    px,
    pr,
    vf,
    ws,
    ka,
    kh,
    kr,
    vc,
    va,
    vl,
    gp,
    gs,
    xr,
    zs,
    zr,
    hg,
    hr,
    s_in, s_hid, r_hid, s_wz, s_wx, r_w, s_k, r_k, s_pc, r_pc, s_pv, r_pv, s_kg, r_kg,
    s_vc, r_vc, s_gx, r_gx, s_gz, r_gz, s_hg, r_hg,
):
    T, n_seq, n_dp, na, nb, halo, R, kv, group = sizes
    C = kv * HD
    Kw = halo + T
    L = n_seq * T
    scale = HD ** -0.5
    W = n_dp * R
    s = lax.axis_index("seq")
    d = lax.axis_index("dp")
    a, b = lax.div(d, nb), lax.rem(d, nb)
    seq_peers = [lax.rem(s + o, n_seq) for o in range(1, n_seq)]
    seq_from = [lax.rem(s + n_seq - o, n_seq) for o in range(1, n_seq)]
    a_peers = [lax.rem(a + o, na) for o in range(1, na)]
    a_from = [lax.rem(a + na - o, na) for o in range(1, na)]
    b_peers = [lax.rem(b + o, nb) for o in range(1, nb)]
    b_from = [lax.rem(b + nb - o, nb) for o in range(1, nb)]

    sends = []

    def rows(i, n):
        return pl.ds(pl.multiple_of(i * n, n), n)

    def copy(src, dst, ss, rs, where):
        return pltpu.make_async_remote_copy(
            src_ref=src, dst_ref=dst, send_sem=ss, recv_sem=rs, device_id=where, device_id_type=MESH
        )

    def start(*args, cond=None):
        if cond is None:
            copy(*args).start()
        else:

            @pl.when(cond)
            def _():
                copy(*args).start()

        sends.append((cond, args))

    def wait_recv(*args, cond=None):
        if cond is None:
            copy(*args).wait_recv()
        else:

            @pl.when(cond)
            def _():
                copy(*args).wait_recv()

    y, core = lax.div(s, 2), lax.rem(s, 2)
    ny = n_seq // 2
    mate = 1 - core
    y_peers = [lax.rem(y + o, ny) for o in range(1, ny)]
    y_from = [lax.rem(y + ny - o, ny) for o in range(1, ny)]

    barrier = pltpu.get_barrier_semaphore()
    for p in seq_peers:
        pl.semaphore_signal(barrier, inc=1, device_id={"seq": p}, device_id_type=MESH)
    for p in a_peers:
        pl.semaphore_signal(barrier, inc=1, device_id={"dp": p * nb + b}, device_id_type=MESH)
    for p in b_peers:
        pl.semaphore_signal(barrier, inc=1, device_id={"dp": a * nb + p}, device_id_type=MESH)

    inputs = [
        (hidden_any, hid),
        (weight_ref.at[rows(s, R), :], wq.at[rows(d, R), :]),
        (key_ref, kf.at[halo:, :]),
        (query_any, query_ref),
        (grad_any, grad_ref),
    ]
    inputs = [pltpu.make_async_copy(x, z, s_in.at[i]) for i, (x, z) in enumerate(inputs)]
    for x in inputs:
        x.start()
    inputs[0].wait()
    for t in range(n_seq):
        if R % 128 == 0:
            for e in range(n_dp):
                at = (e * n_seq + t) * R
                hs[t, :, e * R : (e + 1) * R] = hid[:, at : at + R]
        else:
            hs[t] = hid[t]
    inputs[1].wait()

    pl.semaphore_wait(barrier, n_seq - 1 + na - 1 + nb - 1)

    def w_slot(i):
        return wq.at[rows(i, R), :]

    ahead = jnp.minimum(a + 1, na - 1) * nb + b
    behind = jnp.maximum(a - 1, 0) * nb + b

    def pass_on(i, k, cond=None):
        for o, p in enumerate(b_peers):
            start(w_slot(i), w_slot(i), s_wx.at[k, o], r_w.at[i], {"dp": a * nb + p}, cond=cond)

    start(w_slot(d), w_slot(d), s_wz.at[0, 0], r_w.at[d], {"dp": ahead}, cond=a < na - 1)
    start(w_slot(d), w_slot(d), s_wz.at[0, 1], r_w.at[d], {"dp": behind}, cond=a > 0)
    pass_on(d, 0)

    def hop(k):
        i = jnp.maximum(a - k, 0) * nb + b
        here = a >= k
        wait_recv(w_slot(i), w_slot(i), s_wz.at[k, 0], r_w.at[i], {"dp": d}, cond=here)
        start(
            w_slot(i), w_slot(i), s_wz.at[k, 0], r_w.at[i], {"dp": ahead},
            cond=jnp.logical_and(here, a < na - 1),
        )
        pass_on(i, 2 * k, here)
        i = jnp.minimum(a + k, na - 1) * nb + b
        here = a + k < na
        wait_recv(w_slot(i), w_slot(i), s_wz.at[k, 1], r_w.at[i], {"dp": d}, cond=here)
        start(
            w_slot(i), w_slot(i), s_wz.at[k, 1], r_w.at[i], {"dp": behind},
            cond=jnp.logical_and(here, a > 0),
        )
        pass_on(i, 2 * k + 1, here)

    blocks = []
    left = halo
    while left > 0:
        m = min(T, left)
        blocks.append((left - m, m))
        left -= m
    for o, (at, m) in enumerate(blocks):
        start(
            key_ref.at[T - m :, :], kf.at[at : at + m, :], s_k.at[o], r_k.at[o],
            {"seq": lax.rem(s + o + 1, n_seq)},
        )
    for o, p in enumerate(seq_peers):
        start(hs.at[p], hq.at[rows(s, T), :], s_hid.at[o], r_hid.at[s], {"seq": p})
    hq[rows(s, T), :] = hs[s]

    query_at = s * T + lax.broadcasted_iota(jnp.int32, (Kw, T), 1)
    key_at = s * T - halo + lax.broadcasted_iota(jnp.int32, (Kw, T), 0)
    begin = jnp.zeros((Kw, T), jnp.int32)
    end = jnp.int32(0)
    for i in range(lengths_ref.shape[1]):
        end = end + lengths_ref[0, i]
        begin = jnp.where(query_at >= end, end, begin)
    seen = (key_at >= begin) & (key_at <= query_at)
    bias = jnp.where(seen, 0.0, FAR_NEGATIVE).astype(F32)

    for x in inputs[2:]:
        x.wait()
    for o, (at, m) in enumerate(blocks):
        copy(
            key_ref.at[T - m :, :], kf.at[at : at + m, :], s_k.at[o], r_k.at[o],
            {"seq": lax.rem(s + o + 1, n_seq)},
        ).wait_recv()

    def stack(ref, g):
        return jnp.concatenate(
            [ref[:, pl.ds(pl.multiple_of((g * group + h) * HD, HD), HD)] for h in range(group)], axis=0
        )

    def head(g):
        return pl.ds(pl.multiple_of(g * HD, HD), HD)

    def scores(g, _):
        qs = stack(query_ref, g)
        sc = dot(kf[:, head(g)], qs, 1, 1) * scale + jnp.concatenate([bias] * group, axis=1)
        e = jnp.exp(sc - jnp.max(sc, axis=0, keepdims=True))
        ws[g] = e / jnp.sum(e, axis=0, keepdims=True)
        return 0

    for k in range(max(kv, na - 1)):
        if k < kv:
            scores(k, 0)
        if k < na - 1:
            hop(k + 1)
    for o, p in enumerate(seq_from):
        copy(hs.at[p], hq.at[rows(p, T), :], s_hid.at[o], r_hid.at[p], {"seq": s}).wait_recv()
    for p in b_from:
        for z in range(na):
            i = z * nb + p
            copy(w_slot(i), w_slot(i), s_wx.at[0, 0], r_w.at[i], {"dp": d}).wait_recv()

    pv[:halo, :] = jnp.zeros((halo, C), BF16)

    def project(t, _):
        pv[pl.ds(pl.multiple_of(halo + t * T, 16), T), :] = dot(hq[rows(t, T), :], wq[...], 1, 0).astype(BF16)
        return 0

    lax.fori_loop(0, n_seq, project, 0)

    def pv_rows(t):
        return pv.at[pl.ds(pl.multiple_of(t * T, T), Kw), :]

    for o, p in enumerate(y_peers + [y]):
        start(pv_rows(p * 2 + mate), pc.at[p], s_pc.at[o], r_pc.at[p], {"seq": y * 2 + mate})

    def pair(p):
        copy(pv_rows(p * 2 + core), pc.at[p], s_pc.at[0], r_pc.at[p], {"seq": s}).wait_recv()
        return pv[pl.ds(pl.multiple_of((p * 2 + core) * T, T), Kw), :].astype(F32) + pc[p].astype(F32)

    for o, p in enumerate(y_peers):
        px[p] = pair(p).astype(BF16)
        start(px.at[p], pr.at[y], s_pv.at[o], r_pv.at[y], {"seq": p * 2 + core})
    total = pair(y)
    for o, p in enumerate(y_from):
        copy(px.at[p], pr.at[p], s_pv.at[o], r_pv.at[p], {"seq": s}).wait_recv()
        total = total + pr[p].astype(F32)
    vf[...] = total.astype(BF16)

    def grads(g, _):
        qs = stack(query_ref, g)
        cs = stack(grad_ref, g)
        kg = kf[:, head(g)]
        w = ws[g]
        wl = w.astype(BF16)
        sg = dot(vf[:, head(g)], cs, 1, 1)
        delta = jnp.sum(wl.astype(F32) * sg, axis=0, keepdims=True)
        ds = (w * (sg - delta)).astype(BF16)
        vc[s, :, head(g)] = dot(wl, cs, 1, 0).astype(BF16)
        ka[:, head(g)] = dot(ds, qs, 1, 0) * scale
        qg = (dot(ds, kg, 0, 0) * scale).astype(BF16)
        for h in range(group):
            query_grad_ref[:, pl.ds(pl.multiple_of((g * group + h) * HD, HD), HD)] = qg[h * T : (h + 1) * T]
        return 0

    lax.fori_loop(0, kv, grads, 0)

    saved = pltpu.make_async_copy(query_grad_ref, query_grad_any, s_in.at[0])
    saved.start()
    for o, p in enumerate(y_peers):
        start(vc.at[s], vc.at[s], s_vc.at[o], r_vc.at[s], {"seq": p * 2 + core})
    start(vc.at[s], vc.at[s], s_vc.at[ny - 1], r_vc.at[s], {"seq": y * 2 + mate})
    kh[...] = ka[:halo, :].astype(BF16)
    for o, (at, m) in enumerate(blocks):
        start(
            kh.at[at : at + m, :], kr.at[at : at + m, :], s_kg.at[o], r_kg.at[o],
            {"seq": lax.rem(s + 2 * n_seq - o - 1, n_seq)},
        )
    va[...] = jnp.zeros((halo + L, C), F32)
    for o, p in enumerate(y_from):
        i = p * 2 + core
        copy(vc.at[i], vc.at[i], s_vc.at[o], r_vc.at[i], {"seq": s}).wait_recv()
        start(vc.at[i], vc.at[i], s_vc.at[ny + o], r_vc.at[i], {"seq": y * 2 + mate})
    for p in [y] + y_from:
        i = p * 2 + mate
        copy(vc.at[i], vc.at[i], s_vc.at[0], r_vc.at[i], {"seq": s}).wait_recv()
    for t in range(n_seq):
        va[t * T : t * T + Kw, :] += vc[t].astype(F32)
    vl[...] = va[halo:, :].astype(BF16)

    def send_terms(z):
        for o, p in enumerate(b_peers):
            start(
                gs.at[rows(z * nb + p, R), :], xr.at[b, rows(z, R), :], s_gx.at[z, o], r_gx.at[b, z],
                {"dp": a * nb + p},
            )

    wide = nb * R % 128 == 0
    part = nb * R if wide else W
    for c in range(0, W, part):
        x = dot(hq[:, c : c + part], vl[...], 0, 0)
        gp[c : c + part, :] = x
        gs[c : c + part, :] = x.astype(BF16)
        if wide:
            send_terms(c // part)
    if not wide:
        for z in range(na):
            send_terms(z)

    for o, p in enumerate(seq_peers + [s]):
        x = dot(vl[rows(p, T), :], wq[...], 1, 1).astype(BF16)
        if o < n_seq - 1:
            hg[p] = x
            start(hg.at[p], hr.at[s], s_hg.at[o], r_hg.at[s], {"seq": p})
        else:
            hr[s] = x

    def reduced(z):
        x = gp[rows(z * nb + b, R), :]
        for p in b_from:
            copy(
                gs.at[rows(z * nb + p, R), :], xr.at[p, rows(z, R), :], s_gx.at[0, 0], r_gx.at[p, z],
                {"dp": d},
            ).wait_recv()
            x = x + xr[p, rows(z, R), :].astype(F32)
        return x

    for o, z in enumerate(a_peers):
        zs[z] = reduced(z).astype(BF16)
        start(zs.at[z], zr.at[a], s_gz.at[o], r_gz.at[a], {"dp": z * nb + b})
    mine = reduced(a)

    for o, (at, m) in enumerate(blocks):
        copy(
            kh.at[at : at + m, :], kr.at[at : at + m, :], s_kg.at[o], r_kg.at[o], {"seq": s}
        ).wait_recv()
        ka[Kw - m :, :] += kr[at : at + m, :].astype(F32)
    key_grad_ref[...] = ka[halo:, :].astype(BF16)

    for o, p in enumerate(a_from):
        copy(zs.at[p], zr.at[p], s_gz.at[o], r_gz.at[p], {"dp": d}).wait_recv()
        mine = mine + zr[p].astype(F32)
    weight_grad_ref[...] = mine

    for o, p in enumerate(seq_from):
        copy(hg.at[p], hr.at[p], s_hg.at[o], r_hg.at[p], {"seq": s}).wait_recv()
    for t in range(n_seq):
        if R % 128 == 0:
            for e in range(n_dp):
                at = (e * n_seq + t) * R
                hidden_grad_ref[:, at : at + R] = hr[t, :, e * R : (e + 1) * R]
        else:
            hidden_grad_ref[t] = hr[t]
    saved.wait()
    for cond, args in sends:
        if cond is None:
            copy(*args).wait_send()
        else:

            @pl.when(cond)
            def _():
                copy(*args).wait_send()


def write(*refs):
    n = len(refs) // 2
    sem = refs[-1]
    copies = []
    for x, z in zip(refs[:n], refs[n:-1]):
        many = x.shape[0]
        step = many // 4 if x.shape[-1] > 1024 and many % 64 == 0 else many
        for at in range(0, many, step):
            copies.append(
                pltpu.make_async_copy(x.at[at : at + step], z.at[at : at + step], sem.at[len(copies)])
            )
    for c in copies:
        c.start()
    for c in copies:
        c.wait()


def body(n_dp, n_seq, hidden_states, queries, key_states, context_grad, doc_lengths, value_weight):
    _, T, D = hidden_states.shape
    C = key_states.shape[2]
    kv = C // HD
    group = queries.shape[2] // C
    L = T * n_seq
    halo = min(L, L // 8)
    R = value_weight.shape[0] // n_seq
    na = 4 if n_dp % 4 == 0 else n_dp
    nb = n_dp // na
    W = n_dp * R
    Kw = halo + T
    n_halo = -(-halo // T)
    sizes = (T, n_seq, n_dp, na, nb, halo, R, kv, group)
    hidden = hidden_states[0]
    wide = R % 128 == 0
    if not wide:
        hidden = hidden.reshape(T, n_dp, n_seq, R).transpose(2, 0, 1, 3).reshape(n_seq, T, W)
    vmem = pl.BlockSpec(memory_space=pltpu.VMEM)
    hbm = pl.BlockSpec(memory_space=pl.ANY)
    ny = n_seq // 2
    sem = lambda *shape: pltpu.SemaphoreType.DMA(shape)
    out = pl.pallas_call(
        functools.partial(kernel, sizes),
        out_shape=(
            jax.ShapeDtypeStruct(hidden.shape, BF16),
            jax.ShapeDtypeStruct((T, queries.shape[2]), BF16),
            jax.ShapeDtypeStruct((T, C), BF16),
            jax.ShapeDtypeStruct((R, C), F32),
        ),
        in_specs=[hbm, hbm, hbm, hbm, pl.BlockSpec(memory_space=pltpu.SMEM), hbm],
        out_specs=(vmem, hbm, vmem, vmem),
        scratch_shapes=[
            pltpu.VMEM(hidden.shape, BF16),
            pltpu.VMEM((T, queries.shape[2]), BF16),
            pltpu.VMEM((T, queries.shape[2]), BF16),
            pltpu.VMEM((T, queries.shape[2]), BF16),
            pltpu.VMEM((n_seq, T, W), BF16),
            pltpu.VMEM((L, W), BF16),
            pltpu.VMEM((W, C), BF16),
            pltpu.VMEM((Kw, C), BF16),
            pltpu.VMEM((halo + L, C), BF16),
            pltpu.VMEM((ny, Kw, C), BF16),
            pltpu.VMEM((ny, Kw, C), BF16),
            pltpu.VMEM((ny, Kw, C), BF16),
            pltpu.VMEM((Kw, C), BF16),
            pltpu.VMEM((kv, Kw, group * T), F32),
            pltpu.VMEM((Kw, C), F32),
            pltpu.VMEM((halo, C), BF16),
            pltpu.VMEM((halo, C), BF16),
            pltpu.VMEM((n_seq, Kw, C), BF16),
            pltpu.VMEM((halo + L, C), F32),
            pltpu.VMEM((L, C), BF16),
            pltpu.VMEM((W, C), F32),
            pltpu.VMEM((W, C), BF16),
            pltpu.VMEM((nb, na * R, C), BF16),
            pltpu.VMEM((na, R, C), BF16),
            pltpu.VMEM((na, R, C), BF16),
            pltpu.VMEM((n_seq, T, W), BF16),
            pltpu.VMEM((n_seq, T, W), BF16),
            sem(5), sem(n_seq), sem(n_seq),
            sem(na, 2), sem(2 * na, nb), sem(n_dp),
            sem(n_halo), sem(n_halo),
            sem(ny), sem(ny),
            sem(ny), sem(ny),
            sem(n_halo), sem(n_halo),
            sem(2 * ny), sem(n_seq),
            sem(na, nb), sem(nb, na),
            sem(na), sem(na),
            sem(n_seq), sem(n_seq),
        ],
        compiler_params=pltpu.CompilerParams(
            collective_id=0, has_side_effects=True, vmem_limit_bytes=56 * 1024 * 1024
        ),
        name="attention_backward",
    )(hidden, queries[0], key_states[0], context_grad[0], doc_lengths, value_weight)
    if wide:
        out = pl.pallas_call(
            write,
            out_shape=[jax.ShapeDtypeStruct(x.shape, x.dtype) for x in out],
            in_specs=[hbm] * 4,
            out_specs=[hbm] * 4,
            scratch_shapes=[sem(10)],
            name="write",
        )(*out)
    hidden_grad = out[0]
    if not wide:
        hidden_grad = hidden_grad.reshape(n_seq, T, n_dp, R).transpose(1, 2, 0, 3).reshape(T, D)
    return hidden_grad[None], out[1][None], out[2][None], out[3]


def solution(mesh):
    return jax.shard_map(
        functools.partial(body, mesh.shape["dp"], mesh.shape["seq"]),
        mesh=mesh,
        in_specs=(
            P("dp", "seq", None),
            P("dp", "seq", None),
            P("dp", "seq", None),
            P("dp", "seq", None),
            P("dp", None),
            P("dp", None),
        ),
        out_specs=(
            P("dp", "seq", None),
            P("dp", "seq", None),
            P("dp", "seq", None),
            P(("dp", "seq"), None),
        ),
        check_vma=False,
    )
```

```python
import functools

import jax
import jax.numpy as jnp
from jax import lax
from jax.experimental import pallas as pl
from jax.experimental.pallas import tpu as pltpu
from jax.sharding import PartitionSpec as P

HD = 128
FAR_NEGATIVE = -1e30
MESH = pl.DeviceIdType.MESH
BF16 = jnp.bfloat16
F32 = jnp.float32


def dot(a, b, ca, cb):
    return lax.dot_general(a, b, (((ca,), (cb,)), ((), ())), preferred_element_type=F32)


def kernel(
    sizes,
    hidden_any,
    query_any,
    key_ref,
    grad_any,
    lengths_ref,
    weight_ref,
    hidden_grad_ref,
    query_grad_any,
    key_grad_ref,
    weight_grad_ref,
    hid,
    query_ref,
    grad_ref,
    query_grad_ref,
    hs,
    hq,
    wq,
    kf,
    pv,
    pc,
    px,
    pr,
    vf,
    ws,
    ka,
    kh,
    kr,
    vc,
    va,
    vl,
    gp,
    gs,
    xr,
    zs,
    zr,
    hg,
    hr,
    s_in, s_hid, r_hid, s_wz, s_wx, r_w, s_k, r_k, s_pc, r_pc, s_pv, r_pv, s_kg, r_kg,
    s_vc, r_vc, s_gx, r_gx, s_gz, r_gz, s_hg, r_hg,
):
    T, n_seq, n_dp, na, nb, halo, R, kv, group = sizes
    C = kv * HD
    Kw = halo + T
    L = n_seq * T
    scale = HD ** -0.5
    W = n_dp * R
    s = lax.axis_index("seq")
    d = lax.axis_index("dp")
    a, b = lax.div(d, nb), lax.rem(d, nb)
    seq_peers = [lax.rem(s + o, n_seq) for o in range(1, n_seq)]
    seq_from = [lax.rem(s + n_seq - o, n_seq) for o in range(1, n_seq)]
    a_peers = [lax.rem(a + o, na) for o in range(1, na)]
    a_from = [lax.rem(a + na - o, na) for o in range(1, na)]
    b_peers = [lax.rem(b + o, nb) for o in range(1, nb)]
    b_from = [lax.rem(b + nb - o, nb) for o in range(1, nb)]

    sends = []

    def rows(i, n):
        return pl.ds(pl.multiple_of(i * n, n), n)

    def copy(src, dst, ss, rs, where):
        return pltpu.make_async_remote_copy(
            src_ref=src, dst_ref=dst, send_sem=ss, recv_sem=rs, device_id=where, device_id_type=MESH
        )

    def start(*args, cond=None):
        if cond is None:
            copy(*args).start()
        else:

            @pl.when(cond)
            def _():
                copy(*args).start()

        sends.append((cond, args))

    def wait_recv(*args, cond=None):
        if cond is None:
            copy(*args).wait_recv()
        else:

            @pl.when(cond)
            def _():
                copy(*args).wait_recv()

    y, core = lax.div(s, 2), lax.rem(s, 2)
    ny = n_seq // 2
    mate = 1 - core
    y_peers = [lax.rem(y + o, ny) for o in range(1, ny)]
    y_from = [lax.rem(y + ny - o, ny) for o in range(1, ny)]

    barrier = pltpu.get_barrier_semaphore()
    for p in seq_peers:
        pl.semaphore_signal(barrier, inc=1, device_id={"seq": p}, device_id_type=MESH)
    for p in a_peers:
        pl.semaphore_signal(barrier, inc=1, device_id={"dp": p * nb + b}, device_id_type=MESH)
    for p in b_peers:
        pl.semaphore_signal(barrier, inc=1, device_id={"dp": a * nb + p}, device_id_type=MESH)

    inputs = [
        (hidden_any, hid),
        (weight_ref.at[rows(s, R), :], wq.at[rows(d, R), :]),
        (key_ref, kf.at[halo:, :]),
        (query_any, query_ref),
        (grad_any, grad_ref),
    ]
    inputs = [pltpu.make_async_copy(x, z, s_in.at[i]) for i, (x, z) in enumerate(inputs)]
    for x in inputs:
        x.start()
    inputs[0].wait()
    for t in range(n_seq):
        if R % 128 == 0:
            for e in range(n_dp):
                at = (e * n_seq + t) * R
                hs[t, :, e * R : (e + 1) * R] = hid[:, at : at + R]
        else:
            hs[t] = hid[t]
    inputs[1].wait()

    pl.semaphore_wait(barrier, n_seq - 1 + na - 1 + nb - 1)

    def w_slot(i):
        return wq.at[rows(i, R), :]

    ahead = jnp.minimum(a + 1, na - 1) * nb + b
    behind = jnp.maximum(a - 1, 0) * nb + b

    def pass_on(i, k, cond=None):
        for o, p in enumerate(b_peers):
            start(w_slot(i), w_slot(i), s_wx.at[k, o], r_w.at[i], {"dp": a * nb + p}, cond=cond)

    start(w_slot(d), w_slot(d), s_wz.at[0, 0], r_w.at[d], {"dp": ahead}, cond=a < na - 1)
    start(w_slot(d), w_slot(d), s_wz.at[0, 1], r_w.at[d], {"dp": behind}, cond=a > 0)
    pass_on(d, 0)

    def hop(k):
        i = jnp.maximum(a - k, 0) * nb + b
        here = a >= k
        wait_recv(w_slot(i), w_slot(i), s_wz.at[k, 0], r_w.at[i], {"dp": d}, cond=here)
        start(
            w_slot(i), w_slot(i), s_wz.at[k, 0], r_w.at[i], {"dp": ahead},
            cond=jnp.logical_and(here, a < na - 1),
        )
        pass_on(i, 2 * k, here)
        i = jnp.minimum(a + k, na - 1) * nb + b
        here = a + k < na
        wait_recv(w_slot(i), w_slot(i), s_wz.at[k, 1], r_w.at[i], {"dp": d}, cond=here)
        start(
            w_slot(i), w_slot(i), s_wz.at[k, 1], r_w.at[i], {"dp": behind},
            cond=jnp.logical_and(here, a > 0),
        )
        pass_on(i, 2 * k + 1, here)

    blocks = []
    left = halo
    while left > 0:
        m = min(T, left)
        blocks.append((left - m, m))
        left -= m
    for o, (at, m) in enumerate(blocks):
        start(
            key_ref.at[T - m :, :], kf.at[at : at + m, :], s_k.at[o], r_k.at[o],
            {"seq": lax.rem(s + o + 1, n_seq)},
        )
    for o, p in enumerate(seq_peers):
        start(hs.at[p], hq.at[rows(s, T), :], s_hid.at[o], r_hid.at[s], {"seq": p})
    hq[rows(s, T), :] = hs[s]

    query_at = s * T + lax.broadcasted_iota(jnp.int32, (Kw, T), 1)
    key_at = s * T - halo + lax.broadcasted_iota(jnp.int32, (Kw, T), 0)
    begin = jnp.zeros((Kw, T), jnp.int32)
    end = jnp.int32(0)
    for i in range(lengths_ref.shape[1]):
        end = end + lengths_ref[0, i]
        begin = jnp.where(query_at >= end, end, begin)
    seen = (key_at >= begin) & (key_at <= query_at)
    bias = jnp.where(seen, 0.0, FAR_NEGATIVE).astype(F32)

    for x in inputs[2:]:
        x.wait()
    for o, (at, m) in enumerate(blocks):
        copy(
            key_ref.at[T - m :, :], kf.at[at : at + m, :], s_k.at[o], r_k.at[o],
            {"seq": lax.rem(s + o + 1, n_seq)},
        ).wait_recv()

    def stack(ref, g):
        return jnp.concatenate(
            [ref[:, pl.ds(pl.multiple_of((g * group + h) * HD, HD), HD)] for h in range(group)], axis=0
        )

    def head(g):
        return pl.ds(pl.multiple_of(g * HD, HD), HD)

    def scores(g, _):
        qs = stack(query_ref, g)
        sc = dot(kf[:, head(g)], qs, 1, 1) * scale + jnp.concatenate([bias] * group, axis=1)
        e = jnp.exp(sc - jnp.max(sc, axis=0, keepdims=True))
        ws[g] = e / jnp.sum(e, axis=0, keepdims=True)
        return 0

    for k in range(max(kv, na - 1)):
        if k < kv:
            scores(k, 0)
        if k < na - 1:
            hop(k + 1)
    for o, p in enumerate(seq_from):
        copy(hs.at[p], hq.at[rows(p, T), :], s_hid.at[o], r_hid.at[p], {"seq": s}).wait_recv()
    for p in b_from:
        for z in range(na):
            i = z * nb + p
            copy(w_slot(i), w_slot(i), s_wx.at[0, 0], r_w.at[i], {"dp": d}).wait_recv()

    pv[:halo, :] = jnp.zeros((halo, C), BF16)

    def project(t, _):
        pv[pl.ds(pl.multiple_of(halo + t * T, 16), T), :] = dot(hq[rows(t, T), :], wq[...], 1, 0).astype(BF16)
        return 0

    lax.fori_loop(0, n_seq, project, 0)

    def pv_rows(t):
        return pv.at[pl.ds(pl.multiple_of(t * T, T), Kw), :]

    for o, p in enumerate(y_peers + [y]):
        start(pv_rows(p * 2 + mate), pc.at[p], s_pc.at[o], r_pc.at[p], {"seq": y * 2 + mate})

    def pair(p):
        copy(pv_rows(p * 2 + core), pc.at[p], s_pc.at[0], r_pc.at[p], {"seq": s}).wait_recv()
        return pv[pl.ds(pl.multiple_of((p * 2 + core) * T, T), Kw), :].astype(F32) + pc[p].astype(F32)

    for o, p in enumerate(y_peers):
        px[p] = pair(p).astype(BF16)
        start(px.at[p], pr.at[y], s_pv.at[o], r_pv.at[y], {"seq": p * 2 + core})
    total = pair(y)
    for o, p in enumerate(y_from):
        copy(px.at[p], pr.at[p], s_pv.at[o], r_pv.at[p], {"seq": s}).wait_recv()
        total = total + pr[p].astype(F32)
    vf[...] = total.astype(BF16)

    def grads(g, _):
        qs = stack(query_ref, g)
        cs = stack(grad_ref, g)
        kg = kf[:, head(g)]
        w = ws[g]
        wl = w.astype(BF16)
        sg = dot(vf[:, head(g)], cs, 1, 1)
        delta = jnp.sum(wl.astype(F32) * sg, axis=0, keepdims=True)
        ds = (w * (sg - delta)).astype(BF16)
        vc[s, :, head(g)] = dot(wl, cs, 1, 0).astype(BF16)
        ka[:, head(g)] = dot(ds, qs, 1, 0) * scale
        qg = (dot(ds, kg, 0, 0) * scale).astype(BF16)
        for h in range(group):
            query_grad_ref[:, pl.ds(pl.multiple_of((g * group + h) * HD, HD), HD)] = qg[h * T : (h + 1) * T]
        return 0

    lax.fori_loop(0, kv, grads, 0)

    saved = pltpu.make_async_copy(query_grad_ref, query_grad_any, s_in.at[0])
    saved.start()
    for o, p in enumerate(y_peers):
        start(vc.at[s], vc.at[s], s_vc.at[o], r_vc.at[s], {"seq": p * 2 + core})
    start(vc.at[s], vc.at[s], s_vc.at[ny - 1], r_vc.at[s], {"seq": y * 2 + mate})
    kh[...] = ka[:halo, :].astype(BF16)
    for o, (at, m) in enumerate(blocks):
        start(
            kh.at[at : at + m, :], kr.at[at : at + m, :], s_kg.at[o], r_kg.at[o],
            {"seq": lax.rem(s + 2 * n_seq - o - 1, n_seq)},
        )
    va[...] = jnp.zeros((halo + L, C), F32)
    for o, p in enumerate(y_from):
        i = p * 2 + core
        copy(vc.at[i], vc.at[i], s_vc.at[o], r_vc.at[i], {"seq": s}).wait_recv()
        start(vc.at[i], vc.at[i], s_vc.at[ny + o], r_vc.at[i], {"seq": y * 2 + mate})
    for p in [y] + y_from:
        i = p * 2 + mate
        copy(vc.at[i], vc.at[i], s_vc.at[0], r_vc.at[i], {"seq": s}).wait_recv()
    for t in range(n_seq):
        va[t * T : t * T + Kw, :] += vc[t].astype(F32)
    vl[...] = va[halo:, :].astype(BF16)

    def send_terms(k, z):
        for o, p in enumerate(b_peers):
            start(
                gs.at[rows(z * nb + p, R), :], xr.at[b, rows(z, R), :], s_gx.at[k, o], r_gx.at[b, z],
                {"dp": a * nb + p},
            )

    part = nb * R
    if part % 128 == 0:
        for k, z in enumerate(a_peers + [a]):
            x = dot(hq[:, rows(z, part)], vl[...], 0, 0)
            gp[rows(z, part), :] = x
            gs[rows(z, part), :] = x.astype(BF16)
            send_terms(k, z)
    else:
        x = dot(hq[...], vl[...], 0, 0)
        gp[...] = x
        gs[...] = x.astype(BF16)
        for k, z in enumerate(a_peers + [a]):
            send_terms(k, z)

    for o, p in enumerate(seq_peers + [s]):
        x = dot(vl[rows(p, T), :], wq[...], 1, 1).astype(BF16)
        if o < n_seq - 1:
            hg[p] = x
            start(hg.at[p], hr.at[s], s_hg.at[o], r_hg.at[s], {"seq": p})
        else:
            hr[s] = x

    def reduced(z):
        x = gp[rows(z * nb + b, R), :]
        for p in b_from:
            copy(
                gs.at[rows(z * nb + p, R), :], xr.at[p, rows(z, R), :], s_gx.at[0, 0], r_gx.at[p, z],
                {"dp": d},
            ).wait_recv()
            x = x + xr[p, rows(z, R), :].astype(F32)
        return x

    for o, z in enumerate(a_peers):
        zs[z] = reduced(z).astype(BF16)
        start(zs.at[z], zr.at[a], s_gz.at[o], r_gz.at[a], {"dp": z * nb + b})
    mine = reduced(a)

    for o, (at, m) in enumerate(blocks):
        copy(
            kh.at[at : at + m, :], kr.at[at : at + m, :], s_kg.at[o], r_kg.at[o], {"seq": s}
        ).wait_recv()
        ka[Kw - m :, :] += kr[at : at + m, :].astype(F32)
    key_grad_ref[...] = ka[halo:, :].astype(BF16)

    for o, p in enumerate(a_from):
        copy(zs.at[p], zr.at[p], s_gz.at[o], r_gz.at[p], {"dp": d}).wait_recv()
        mine = mine + zr[p].astype(F32)
    weight_grad_ref[...] = mine

    for o, p in enumerate(seq_from):
        copy(hg.at[p], hr.at[p], s_hg.at[o], r_hg.at[p], {"seq": s}).wait_recv()
    for t in range(n_seq):
        if R % 128 == 0:
            for e in range(n_dp):
                at = (e * n_seq + t) * R
                hidden_grad_ref[:, at : at + R] = hr[t, :, e * R : (e + 1) * R]
        else:
            hidden_grad_ref[t] = hr[t]
    saved.wait()
    for cond, args in sends:
        if cond is None:
            copy(*args).wait_send()
        else:

            @pl.when(cond)
            def _():
                copy(*args).wait_send()


def write(*refs):
    n = len(refs) // 2
    for x, z in zip(refs[:n], refs[n:]):
        z[...] = x[...]


def body(n_dp, n_seq, hidden_states, queries, key_states, context_grad, doc_lengths, value_weight):
    _, T, D = hidden_states.shape
    C = key_states.shape[2]
    kv = C // HD
    group = queries.shape[2] // C
    L = T * n_seq
    halo = min(L, L // 8)
    R = value_weight.shape[0] // n_seq
    na = 4 if n_dp % 4 == 0 else n_dp
    nb = n_dp // na
    W = n_dp * R
    Kw = halo + T
    n_halo = -(-halo // T)
    sizes = (T, n_seq, n_dp, na, nb, halo, R, kv, group)
    hidden = hidden_states[0]
    wide = R % 128 == 0
    if not wide:
        hidden = hidden.reshape(T, n_dp, n_seq, R).transpose(2, 0, 1, 3).reshape(n_seq, T, W)
    vmem = pl.BlockSpec(memory_space=pltpu.VMEM)
    hbm = pl.BlockSpec(memory_space=pl.ANY)
    ny = n_seq // 2
    sem = lambda *shape: pltpu.SemaphoreType.DMA(shape)
    out = pl.pallas_call(
        functools.partial(kernel, sizes),
        out_shape=(
            jax.ShapeDtypeStruct(hidden.shape, BF16),
            jax.ShapeDtypeStruct((T, queries.shape[2]), BF16),
            jax.ShapeDtypeStruct((T, C), BF16),
            jax.ShapeDtypeStruct((R, C), F32),
        ),
        in_specs=[hbm, hbm, hbm, hbm, pl.BlockSpec(memory_space=pltpu.SMEM), hbm],
        out_specs=(vmem, hbm, vmem, vmem),
        scratch_shapes=[
            pltpu.VMEM(hidden.shape, BF16),
            pltpu.VMEM((T, queries.shape[2]), BF16),
            pltpu.VMEM((T, queries.shape[2]), BF16),
            pltpu.VMEM((T, queries.shape[2]), BF16),
            pltpu.VMEM((n_seq, T, W), BF16),
            pltpu.VMEM((L, W), BF16),
            pltpu.VMEM((W, C), BF16),
            pltpu.VMEM((Kw, C), BF16),
            pltpu.VMEM((halo + L, C), BF16),
            pltpu.VMEM((ny, Kw, C), BF16),
            pltpu.VMEM((ny, Kw, C), BF16),
            pltpu.VMEM((ny, Kw, C), BF16),
            pltpu.VMEM((Kw, C), BF16),
            pltpu.VMEM((kv, Kw, group * T), F32),
            pltpu.VMEM((Kw, C), F32),
            pltpu.VMEM((halo, C), BF16),
            pltpu.VMEM((halo, C), BF16),
            pltpu.VMEM((n_seq, Kw, C), BF16),
            pltpu.VMEM((halo + L, C), F32),
            pltpu.VMEM((L, C), BF16),
            pltpu.VMEM((W, C), F32),
            pltpu.VMEM((W, C), BF16),
            pltpu.VMEM((nb, na * R, C), BF16),
            pltpu.VMEM((na, R, C), BF16),
            pltpu.VMEM((na, R, C), BF16),
            pltpu.VMEM((n_seq, T, W), BF16),
            pltpu.VMEM((n_seq, T, W), BF16),
            sem(5), sem(n_seq), sem(n_seq),
            sem(na, 2), sem(2 * na, nb), sem(n_dp),
            sem(n_halo), sem(n_halo),
            sem(ny), sem(ny),
            sem(ny), sem(ny),
            sem(n_halo), sem(n_halo),
            sem(2 * ny), sem(n_seq),
            sem(na, nb), sem(nb, na),
            sem(na), sem(na),
            sem(n_seq), sem(n_seq),
        ],
        compiler_params=pltpu.CompilerParams(
            collective_id=0, has_side_effects=True, vmem_limit_bytes=56 * 1024 * 1024
        ),
        name="attention_backward",
    )(hidden, queries[0], key_states[0], context_grad[0], doc_lengths, value_weight)
    if wide:
        blocks = [pl.BlockSpec((x.shape[0] // 4, x.shape[1]), lambda i: (i, 0)) for x in out]
        out = pl.pallas_call(
            write,
            grid=(4,),
            out_shape=[jax.ShapeDtypeStruct(x.shape, x.dtype) for x in out],
            in_specs=blocks,
            out_specs=blocks,
            name="write",
        )(*out)
    hidden_grad = out[0]
    if not wide:
        hidden_grad = hidden_grad.reshape(n_seq, T, n_dp, R).transpose(1, 2, 0, 3).reshape(T, D)
    return hidden_grad[None], out[1][None], out[2][None], out[3]


def solution(mesh):
    return jax.shard_map(
        functools.partial(body, mesh.shape["dp"], mesh.shape["seq"]),
        mesh=mesh,
        in_specs=(
            P("dp", "seq", None),
            P("dp", "seq", None),
            P("dp", "seq", None),
            P("dp", "seq", None),
            P("dp", None),
            P("dp", None),
        ),
        out_specs=(
            P("dp", "seq", None),
            P("dp", "seq", None),
            P("dp", "seq", None),
            P(("dp", "seq"), None),
        ),
        check_vma=False,
    )
```

```python
import functools

import jax
import jax.numpy as jnp
from jax import lax
from jax.experimental import pallas as pl
from jax.experimental.pallas import tpu as pltpu
from jax.sharding import PartitionSpec as P

HD = 128
FAR_NEGATIVE = -1e30
MESH = pl.DeviceIdType.MESH
BF16 = jnp.bfloat16
F32 = jnp.float32


def dot(a, b, ca, cb):
    return lax.dot_general(a, b, (((ca,), (cb,)), ((), ())), preferred_element_type=F32)


def kernel(
    sizes,
    hidden_any,
    query_any,
    key_ref,
    grad_any,
    lengths_ref,
    weight_ref,
    hidden_grad_ref,
    query_grad_any,
    key_grad_ref,
    weight_grad_ref,
    hid,
    query_ref,
    grad_ref,
    query_grad_ref,
    hs,
    hq,
    wq,
    kf,
    pv,
    pc,
    px,
    pr,
    vf,
    ws,
    ka,
    kh,
    kr,
    vc,
    va,
    vl,
    gp,
    gs,
    xr,
    zs,
    zr,
    hg,
    hr,
    s_in, s_hid, r_hid, s_wz, s_wx, r_w, s_k, r_k, s_pc, r_pc, s_pv, r_pv, s_kg, r_kg,
    s_vc, r_vc, s_gx, r_gx, s_gz, r_gz, s_hg, r_hg,
):
    T, n_seq, n_dp, na, nb, halo, R, kv, group = sizes
    C = kv * HD
    Kw = halo + T
    L = n_seq * T
    scale = HD ** -0.5
    W = n_dp * R
    s = lax.axis_index("seq")
    d = lax.axis_index("dp")
    a, b = lax.div(d, nb), lax.rem(d, nb)
    seq_peers = [lax.rem(s + o, n_seq) for o in range(1, n_seq)]
    seq_from = [lax.rem(s + n_seq - o, n_seq) for o in range(1, n_seq)]
    a_peers = [lax.rem(a + o, na) for o in range(1, na)]
    a_from = [lax.rem(a + na - o, na) for o in range(1, na)]
    far = lax.rem(a + 2, na)
    a_order = [far, far + 1 - 2 * lax.rem(far, 2), a + 1 - 2 * lax.rem(a, 2)] if na == 4 else a_peers
    b_peers = [lax.rem(b + o, nb) for o in range(1, nb)]
    b_from = [lax.rem(b + nb - o, nb) for o in range(1, nb)]

    sends = []

    def rows(i, n):
        return pl.ds(pl.multiple_of(i * n, n), n)

    def copy(src, dst, ss, rs, where):
        return pltpu.make_async_remote_copy(
            src_ref=src, dst_ref=dst, send_sem=ss, recv_sem=rs, device_id=where, device_id_type=MESH
        )

    def start(*args, cond=None):
        if cond is None:
            copy(*args).start()
        else:

            @pl.when(cond)
            def _():
                copy(*args).start()

        sends.append((cond, args))

    def wait_recv(*args, cond=None):
        if cond is None:
            copy(*args).wait_recv()
        else:

            @pl.when(cond)
            def _():
                copy(*args).wait_recv()

    y, core = lax.div(s, 2), lax.rem(s, 2)
    ny = n_seq // 2
    mate = 1 - core
    y_peers = [lax.rem(y + o, ny) for o in range(1, ny)]
    y_from = [lax.rem(y + ny - o, ny) for o in range(1, ny)]

    barrier = pltpu.get_barrier_semaphore()
    for p in seq_peers:
        pl.semaphore_signal(barrier, inc=1, device_id={"seq": p}, device_id_type=MESH)
    for p in a_peers:
        pl.semaphore_signal(barrier, inc=1, device_id={"dp": p * nb + b}, device_id_type=MESH)
    for p in b_peers:
        pl.semaphore_signal(barrier, inc=1, device_id={"dp": a * nb + p}, device_id_type=MESH)

    inputs = [
        (hidden_any, hid),
        (weight_ref.at[rows(s, R), :], wq.at[rows(d, R), :]),
        (key_ref, kf.at[halo:, :]),
        (query_any, query_ref),
        (grad_any, grad_ref),
    ]
    inputs = [pltpu.make_async_copy(x, z, s_in.at[i]) for i, (x, z) in enumerate(inputs)]
    for x in inputs:
        x.start()
    inputs[0].wait()
    for t in range(n_seq):
        if R % 128 == 0:
            for e in range(n_dp):
                at = (e * n_seq + t) * R
                hs[t, :, e * R : (e + 1) * R] = hid[:, at : at + R]
        else:
            hs[t] = hid[t]
    inputs[1].wait()

    pl.semaphore_wait(barrier, n_seq - 1 + na - 1 + nb - 1)

    def w_slot(i):
        return wq.at[rows(i, R), :]

    ahead = jnp.minimum(a + 1, na - 1) * nb + b
    behind = jnp.maximum(a - 1, 0) * nb + b

    def pass_on(i, k, cond=None):
        for o, p in enumerate(b_peers):
            start(w_slot(i), w_slot(i), s_wx.at[k, o], r_w.at[i], {"dp": a * nb + p}, cond=cond)

    start(w_slot(d), w_slot(d), s_wz.at[0, 0], r_w.at[d], {"dp": ahead}, cond=a < na - 1)
    start(w_slot(d), w_slot(d), s_wz.at[0, 1], r_w.at[d], {"dp": behind}, cond=a > 0)
    pass_on(d, 0)

    def hop(k):
        i = jnp.maximum(a - k, 0) * nb + b
        here = a >= k
        wait_recv(w_slot(i), w_slot(i), s_wz.at[k, 0], r_w.at[i], {"dp": d}, cond=here)
        start(
            w_slot(i), w_slot(i), s_wz.at[k, 0], r_w.at[i], {"dp": ahead},
            cond=jnp.logical_and(here, a < na - 1),
        )
        pass_on(i, 2 * k, here)
        i = jnp.minimum(a + k, na - 1) * nb + b
        here = a + k < na
        wait_recv(w_slot(i), w_slot(i), s_wz.at[k, 1], r_w.at[i], {"dp": d}, cond=here)
        start(
            w_slot(i), w_slot(i), s_wz.at[k, 1], r_w.at[i], {"dp": behind},
            cond=jnp.logical_and(here, a > 0),
        )
        pass_on(i, 2 * k + 1, here)

    blocks = []
    left = halo
    while left > 0:
        m = min(T, left)
        blocks.append((left - m, m))
        left -= m
    for o, (at, m) in enumerate(blocks):
        start(
            key_ref.at[T - m :, :], kf.at[at : at + m, :], s_k.at[o], r_k.at[o],
            {"seq": lax.rem(s + o + 1, n_seq)},
        )
    for o, p in enumerate(seq_peers):
        start(hs.at[p], hq.at[rows(s, T), :], s_hid.at[o], r_hid.at[s], {"seq": p})
    hq[rows(s, T), :] = hs[s]

    query_at = s * T + lax.broadcasted_iota(jnp.int32, (Kw, T), 1)
    key_at = s * T - halo + lax.broadcasted_iota(jnp.int32, (Kw, T), 0)
    begin = jnp.zeros((Kw, T), jnp.int32)
    end = jnp.int32(0)
    for i in range(lengths_ref.shape[1]):
        end = end + lengths_ref[0, i]
        begin = jnp.where(query_at >= end, end, begin)
    seen = (key_at >= begin) & (key_at <= query_at)
    bias = jnp.where(seen, 0.0, FAR_NEGATIVE).astype(F32)

    for x in inputs[2:]:
        x.wait()
    for o, (at, m) in enumerate(blocks):
        copy(
            key_ref.at[T - m :, :], kf.at[at : at + m, :], s_k.at[o], r_k.at[o],
            {"seq": lax.rem(s + o + 1, n_seq)},
        ).wait_recv()

    def stack(ref, g):
        return jnp.concatenate(
            [ref[:, pl.ds(pl.multiple_of((g * group + h) * HD, HD), HD)] for h in range(group)], axis=0
        )

    def head(g):
        return pl.ds(pl.multiple_of(g * HD, HD), HD)

    def scores(g, _):
        qs = stack(query_ref, g)
        sc = dot(kf[:, head(g)], qs, 1, 1) * scale + jnp.concatenate([bias] * group, axis=1)
        e = jnp.exp(sc - jnp.max(sc, axis=0, keepdims=True))
        ws[g] = e / jnp.sum(e, axis=0, keepdims=True)
        return 0

    for k in range(max(kv, na - 1)):
        if k < kv:
            scores(k, 0)
        if k < na - 1:
            hop(k + 1)
    for o, p in enumerate(seq_from):
        copy(hs.at[p], hq.at[rows(p, T), :], s_hid.at[o], r_hid.at[p], {"seq": s}).wait_recv()
    for p in b_from:
        for z in range(na):
            i = z * nb + p
            copy(w_slot(i), w_slot(i), s_wx.at[0, 0], r_w.at[i], {"dp": d}).wait_recv()

    pv[:halo, :] = jnp.zeros((halo, C), BF16)

    def project(t, _):
        pv[pl.ds(pl.multiple_of(halo + t * T, 16), T), :] = dot(hq[rows(t, T), :], wq[...], 1, 0).astype(BF16)
        return 0

    lax.fori_loop(0, n_seq, project, 0)

    def pv_rows(t):
        return pv.at[pl.ds(pl.multiple_of(t * T, T), Kw), :]

    for o, p in enumerate(y_peers + [y]):
        start(pv_rows(p * 2 + mate), pc.at[p], s_pc.at[o], r_pc.at[p], {"seq": y * 2 + mate})

    def pair(p):
        copy(pv_rows(p * 2 + core), pc.at[p], s_pc.at[0], r_pc.at[p], {"seq": s}).wait_recv()
        return pv[pl.ds(pl.multiple_of((p * 2 + core) * T, T), Kw), :].astype(F32) + pc[p].astype(F32)

    for o, p in enumerate(y_peers):
        px[p] = pair(p).astype(BF16)
        start(px.at[p], pr.at[y], s_pv.at[o], r_pv.at[y], {"seq": p * 2 + core})
    total = pair(y)
    for o, p in enumerate(y_from):
        copy(px.at[p], pr.at[p], s_pv.at[o], r_pv.at[p], {"seq": s}).wait_recv()
        total = total + pr[p].astype(F32)
    vf[...] = total.astype(BF16)

    def grads(g, _):
        qs = stack(query_ref, g)
        cs = stack(grad_ref, g)
        kg = kf[:, head(g)]
        w = ws[g]
        wl = w.astype(BF16)
        sg = dot(vf[:, head(g)], cs, 1, 1)
        delta = jnp.sum(wl.astype(F32) * sg, axis=0, keepdims=True)
        ds = (w * (sg - delta)).astype(BF16)
        vc[s, :, head(g)] = dot(wl, cs, 1, 0).astype(BF16)
        ka[:, head(g)] = dot(ds, qs, 1, 0) * scale
        qg = (dot(ds, kg, 0, 0) * scale).astype(BF16)
        for h in range(group):
            query_grad_ref[:, pl.ds(pl.multiple_of((g * group + h) * HD, HD), HD)] = qg[h * T : (h + 1) * T]
        return 0

    lax.fori_loop(0, kv, grads, 0)

    saved = pltpu.make_async_copy(query_grad_ref, query_grad_any, s_in.at[0])
    saved.start()
    for o, p in enumerate(y_peers):
        start(vc.at[s], vc.at[s], s_vc.at[o], r_vc.at[s], {"seq": p * 2 + core})
    start(vc.at[s], vc.at[s], s_vc.at[ny - 1], r_vc.at[s], {"seq": y * 2 + mate})
    kh[...] = ka[:halo, :].astype(BF16)
    for o, (at, m) in enumerate(blocks):
        start(
            kh.at[at : at + m, :], kr.at[at : at + m, :], s_kg.at[o], r_kg.at[o],
            {"seq": lax.rem(s + 2 * n_seq - o - 1, n_seq)},
        )
    va[...] = jnp.zeros((halo + L, C), F32)
    for o, p in enumerate(y_from):
        i = p * 2 + core
        copy(vc.at[i], vc.at[i], s_vc.at[o], r_vc.at[i], {"seq": s}).wait_recv()
        start(vc.at[i], vc.at[i], s_vc.at[ny + o], r_vc.at[i], {"seq": y * 2 + mate})
    for p in [y] + y_from:
        i = p * 2 + mate
        copy(vc.at[i], vc.at[i], s_vc.at[0], r_vc.at[i], {"seq": s}).wait_recv()
    for t in range(n_seq):
        va[t * T : t * T + Kw, :] += vc[t].astype(F32)
    vl[...] = va[halo:, :].astype(BF16)

    def send_terms(k, z):
        for o, p in enumerate(b_peers):
            start(
                gs.at[rows(z * nb + p, R), :], xr.at[b, rows(z, R), :], s_gx.at[k, o], r_gx.at[b, z],
                {"dp": a * nb + p},
            )

    part = nb * R
    if part % 128 == 0:
        for k, z in enumerate(a_order + [a]):
            x = dot(hq[:, rows(z, part)], vl[...], 0, 0)
            gp[rows(z, part), :] = x
            gs[rows(z, part), :] = x.astype(BF16)
            send_terms(k, z)
    else:
        x = dot(hq[...], vl[...], 0, 0)
        gp[...] = x
        gs[...] = x.astype(BF16)
        for k, z in enumerate(a_order + [a]):
            send_terms(k, z)

    for o, p in enumerate(seq_peers + [s]):
        x = dot(vl[rows(p, T), :], wq[...], 1, 1).astype(BF16)
        if o < n_seq - 1:
            hg[p] = x
            start(hg.at[p], hr.at[s], s_hg.at[o], r_hg.at[s], {"seq": p})
        else:
            hr[s] = x

    def reduced(z):
        x = gp[rows(z * nb + b, R), :]
        for p in b_from:
            copy(
                gs.at[rows(z * nb + p, R), :], xr.at[p, rows(z, R), :], s_gx.at[0, 0], r_gx.at[p, z],
                {"dp": d},
            ).wait_recv()
            x = x + xr[p, rows(z, R), :].astype(F32)
        return x

    for o, z in enumerate(a_order):
        zs[z] = reduced(z).astype(BF16)
        start(zs.at[z], zr.at[a], s_gz.at[o], r_gz.at[a], {"dp": z * nb + b})
    mine = reduced(a)

    for o, (at, m) in enumerate(blocks):
        copy(
            kh.at[at : at + m, :], kr.at[at : at + m, :], s_kg.at[o], r_kg.at[o], {"seq": s}
        ).wait_recv()
        ka[Kw - m :, :] += kr[at : at + m, :].astype(F32)
    key_grad_ref[...] = ka[halo:, :].astype(BF16)

    for o, p in enumerate(a_from):
        copy(zs.at[p], zr.at[p], s_gz.at[o], r_gz.at[p], {"dp": d}).wait_recv()
        mine = mine + zr[p].astype(F32)
    weight_grad_ref[...] = mine

    for o, p in enumerate(seq_from):
        copy(hg.at[p], hr.at[p], s_hg.at[o], r_hg.at[p], {"seq": s}).wait_recv()
    for t in range(n_seq):
        if R % 128 == 0:
            for e in range(n_dp):
                at = (e * n_seq + t) * R
                hidden_grad_ref[:, at : at + R] = hr[t, :, e * R : (e + 1) * R]
        else:
            hidden_grad_ref[t] = hr[t]
    saved.wait()
    for cond, args in sends:
        if cond is None:
            copy(*args).wait_send()
        else:

            @pl.when(cond)
            def _():
                copy(*args).wait_send()


def write(*refs):
    n = len(refs) // 2
    for x, z in zip(refs[:n], refs[n:]):
        z[...] = x[...]


def body(n_dp, n_seq, hidden_states, queries, key_states, context_grad, doc_lengths, value_weight):
    _, T, D = hidden_states.shape
    C = key_states.shape[2]
    kv = C // HD
    group = queries.shape[2] // C
    L = T * n_seq
    halo = min(L, L // 8)
    R = value_weight.shape[0] // n_seq
    na = 4 if n_dp % 4 == 0 else n_dp
    nb = n_dp // na
    W = n_dp * R
    Kw = halo + T
    n_halo = -(-halo // T)
    sizes = (T, n_seq, n_dp, na, nb, halo, R, kv, group)
    hidden = hidden_states[0]
    wide = R % 128 == 0
    if not wide:
        hidden = hidden.reshape(T, n_dp, n_seq, R).transpose(2, 0, 1, 3).reshape(n_seq, T, W)
    vmem = pl.BlockSpec(memory_space=pltpu.VMEM)
    hbm = pl.BlockSpec(memory_space=pl.ANY)
    ny = n_seq // 2
    sem = lambda *shape: pltpu.SemaphoreType.DMA(shape)
    out = pl.pallas_call(
        functools.partial(kernel, sizes),
        out_shape=(
            jax.ShapeDtypeStruct(hidden.shape, BF16),
            jax.ShapeDtypeStruct((T, queries.shape[2]), BF16),
            jax.ShapeDtypeStruct((T, C), BF16),
            jax.ShapeDtypeStruct((R, C), F32),
        ),
        in_specs=[hbm, hbm, hbm, hbm, pl.BlockSpec(memory_space=pltpu.SMEM), hbm],
        out_specs=(vmem, hbm, vmem, vmem),
        scratch_shapes=[
            pltpu.VMEM(hidden.shape, BF16),
            pltpu.VMEM((T, queries.shape[2]), BF16),
            pltpu.VMEM((T, queries.shape[2]), BF16),
            pltpu.VMEM((T, queries.shape[2]), BF16),
            pltpu.VMEM((n_seq, T, W), BF16),
            pltpu.VMEM((L, W), BF16),
            pltpu.VMEM((W, C), BF16),
            pltpu.VMEM((Kw, C), BF16),
            pltpu.VMEM((halo + L, C), BF16),
            pltpu.VMEM((ny, Kw, C), BF16),
            pltpu.VMEM((ny, Kw, C), BF16),
            pltpu.VMEM((ny, Kw, C), BF16),
            pltpu.VMEM((Kw, C), BF16),
            pltpu.VMEM((kv, Kw, group * T), F32),
            pltpu.VMEM((Kw, C), F32),
            pltpu.VMEM((halo, C), BF16),
            pltpu.VMEM((halo, C), BF16),
            pltpu.VMEM((n_seq, Kw, C), BF16),
            pltpu.VMEM((halo + L, C), F32),
            pltpu.VMEM((L, C), BF16),
            pltpu.VMEM((W, C), F32),
            pltpu.VMEM((W, C), BF16),
            pltpu.VMEM((nb, na * R, C), BF16),
            pltpu.VMEM((na, R, C), BF16),
            pltpu.VMEM((na, R, C), BF16),
            pltpu.VMEM((n_seq, T, W), BF16),
            pltpu.VMEM((n_seq, T, W), BF16),
            sem(5), sem(n_seq), sem(n_seq),
            sem(na, 2), sem(2 * na, nb), sem(n_dp),
            sem(n_halo), sem(n_halo),
            sem(ny), sem(ny),
            sem(ny), sem(ny),
            sem(n_halo), sem(n_halo),
            sem(2 * ny), sem(n_seq),
            sem(na, nb), sem(nb, na),
            sem(na), sem(na),
            sem(n_seq), sem(n_seq),
        ],
        compiler_params=pltpu.CompilerParams(
            collective_id=0, has_side_effects=True, vmem_limit_bytes=56 * 1024 * 1024
        ),
        name="attention_backward",
    )(hidden, queries[0], key_states[0], context_grad[0], doc_lengths, value_weight)
    if wide:
        blocks = [pl.BlockSpec((x.shape[0] // 2, x.shape[1]), lambda i: (i, 0)) for x in out]
        out = pl.pallas_call(
            write,
            grid=(2,),
            out_shape=[jax.ShapeDtypeStruct(x.shape, x.dtype) for x in out],
            in_specs=blocks,
            out_specs=blocks,
            name="write",
        )(*out)
    hidden_grad = out[0]
    if not wide:
        hidden_grad = hidden_grad.reshape(n_seq, T, n_dp, R).transpose(1, 2, 0, 3).reshape(T, D)
    return hidden_grad[None], out[1][None], out[2][None], out[3]


def solution(mesh):
    return jax.shard_map(
        functools.partial(body, mesh.shape["dp"], mesh.shape["seq"]),
        mesh=mesh,
        in_specs=(
            P("dp", "seq", None),
            P("dp", "seq", None),
            P("dp", "seq", None),
            P("dp", "seq", None),
            P("dp", None),
            P("dp", None),
        ),
        out_specs=(
            P("dp", "seq", None),
            P("dp", "seq", None),
            P("dp", "seq", None),
            P(("dp", "seq"), None),
        ),
        check_vma=False,
    )
```
